32 devices in a mesh: section: 2 (over core), ctx: 16 (over z, y, x).
Axes of the slice: x: 2, y: 2, z: 4, core: 2. Of those that a mesh axis runs over, the one named last changes fastest.
Arguments:
- hidden_in: bfloat16 [4096, 8192], P('ctx'), may hold values from -3 to 3
- query_rows: bfloat16 [2, 4096, 8192], P('section', 'ctx'), may hold values from -6 to 6
- key_rows: bfloat16 [2, 4096, 1024], P('section', 'ctx'), may hold values from -6 to 6
- value_rows: bfloat16 [2, 4096, 1024], P('section', 'ctx'), may hold values from -24 to 24
- stretch_len: int32 [16], replicated, may hold values from 128 to 256, as said below
- segment_ids: int32 [4096], P('ctx'), may hold values from 0 to 34, as said below
Outputs:
- hidden_out: bfloat16 [2, 4096, 8192], P('section', 'ctx')
The draws below stay inside these ranges and needn't reach their ends.
Inputs may be any that keep to these rules, and one draw needn't show every extreme that they name: stretch_len values are multiples of 128; stretch_len[0] = 256 and the last entry is 128. `segment_ids`: segment ids never fall along the slots; exactly the first 128 slots carry 0; each candidate solution covers at most 1536 consecutive slots, and one covers exactly that many; the last slot carries the largest id.
All inputs are finite; a program needn't handle non-finite values.
Results may differ from the reference program's by a relative error of at most 0.005.
Values may be sent and summed in bfloat16 or wider, within the bound.
A program may use at most 320 MiB of HBM per device.

```python
import jax
import jax.numpy as jnp
from jax import lax

D = 8192
QH = 64
KVH = 8
HD = 128
TOK_DEV = 256
PROMPT = 128
REACH = 6
GRAIN = 128
TOKENS = 4096


def draw_query_rows(key, part):
    key = jax.random.fold_in(key, 3)
    base_draw = jnp.clip(jax.random.normal(key, (2, TOKENS, D), jnp.float32), -6.0, 6.0)
    return base_draw.astype(jnp.bfloat16)


def draw_key_rows(key, part):
    key = jax.random.fold_in(key, 5)
    base_draw = jnp.clip(jax.random.normal(key, (2, TOKENS, KVH * HD), jnp.float32), -6.0, 6.0)
    return base_draw.astype(jnp.bfloat16)


def draw_stretch_len(key, part):
    key = jax.random.fold_in(key, 7)
    count = TOKENS // TOK_DEV
    granules = jax.random.randint(key, (count,), 1, TOK_DEV // GRAIN + 1)
    lengths = granules * GRAIN
    lengths = lengths.at[0].set(TOK_DEV)
    lengths = lengths.at[count - 1].set(GRAIN)
    return lengths.astype(jnp.int32)


def draw_segment_ids(key, part):
    key = jax.random.fold_in(key, 11)
    count = 2 * (TOKENS // TOK_DEV) + 2
    lengths = jax.random.randint(key, (count,), 2 * TOK_DEV, REACH * TOK_DEV + 1)
    lengths = lengths.at[0].set(REACH * TOK_DEV)
    starts = PROMPT + jnp.cumsum(lengths) - lengths
    slot_index = jnp.arange(TOKENS, dtype=jnp.int32)
    ids = jnp.sum((slot_index[:, None] >= starts[None, :]).astype(jnp.int32), axis=1)
    ids = ids.at[TOKENS - 1].set(count)
    return ids.astype(jnp.int32)


def levels(own_key, dims, split, low, high):
    def one(dim, blocks):
        draws = jax.random.uniform(jax.random.fold_in(jax.random.fold_in(own_key, 6), dim), (blocks,), jnp.float32, low / len(split), high / len(split))
        return jnp.repeat(jnp.exp(draws), dims[dim] // blocks).reshape((-1,) + (1,) * (len(dims) - dim - 1))

    gain = one(*split[0])
    for cut in split[1:]:
        gain = gain * one(*cut)
    return gain


def scatter_about(key, dims, scale, reach, cuts=(), kind=jnp.bfloat16):
    factor_of = levels(key, dims, cuts, -0.22, 0.18) if cuts else 1.0
    result = jax.random.normal(key, dims, jnp.float32) * scale * factor_of
    return jnp.minimum(jnp.maximum(result, -reach), reach).astype(kind)


def setup_inputs(seed: int = 0) -> dict:
    splits = jax.random.split(jax.random.key(seed), 7)
    hidden_in = scatter_about(splits[0], (TOKENS, D), 0.5, 3.0, ((0, 16),))
    query_rows = draw_query_rows(jax.random.fold_in(splits[6], 71), 0)
    key_rows = draw_key_rows(jax.random.fold_in(splits[6], 71), 0)
    value_rows = scatter_about(splits[3], (2, TOKENS, KVH * HD), 4.0, 24.0, ((0, 2), (1, 16)))
    stretch_len = draw_stretch_len(jax.random.fold_in(splits[6], 71), 0)
    segment_ids = draw_segment_ids(jax.random.fold_in(splits[6], 71), 0)
    return {"hidden_in": hidden_in, "query_rows": query_rows, "key_rows": key_rows, "value_rows": value_rows, "stretch_len": stretch_len, "segment_ids": segment_ids}


NEG_FILL = -1e30


def softmax_context(query_block, key_block, value_block, visible):
    count = query_block.shape[0]
    query_heads = query_block.astype(jnp.float32).reshape(count, KVH, QH // KVH, HD)
    key_heads = key_block.astype(jnp.float32).reshape(key_block.shape[0], KVH, HD)
    value_heads = value_block.astype(jnp.float32).reshape(value_block.shape[0], KVH, HD)
    scores = jnp.einsum("tkgd,skd->kgts", query_heads, key_heads) * (HD ** -0.5)
    scores = jnp.where(visible, scores, NEG_FILL)
    top_score = jnp.max(scores, axis=-1, keepdims=True)
    weights = jnp.where(visible, jnp.exp(scores - top_score), 0.0)
    totals = jnp.sum(weights, axis=-1)
    rounded = lax.optimization_barrier(weights.astype(jnp.bfloat16)).astype(jnp.float32)
    mixed_sum = jnp.einsum("kgts,skd->tkgd", rounded, value_heads)
    context = mixed_sum / jnp.transpose(totals, (2, 0, 1))[..., None]
    return context.reshape(count, D)


def section_layer(query_all, key_all, value_all, slot_valid, segment_ids):
    back_span = REACH * TOK_DEV
    width = key_all.shape[1]
    pad_keys = jnp.concatenate([jnp.zeros((back_span, width), key_all.dtype), key_all])
    pad_values = jnp.concatenate([jnp.zeros((back_span, width), value_all.dtype), value_all])
    pad_valid = jnp.concatenate([jnp.zeros((back_span,), jnp.int32), slot_valid])
    pad_segments = jnp.concatenate([jnp.zeros((back_span,), jnp.int32), segment_ids])
    prompt_keys = key_all[:TOK_DEV]
    prompt_values = value_all[:TOK_DEV]
    prompt_valid = slot_valid[:TOK_DEV] > 0
    prompt_segments = segment_ids[:TOK_DEV]

    def one_stretch(device):
        first_row = device * TOK_DEV
        query_block = lax.dynamic_slice_in_dim(query_all, first_row, TOK_DEV, 0)
        query_valid = lax.dynamic_slice_in_dim(slot_valid, first_row, TOK_DEV, 0) > 0
        query_segments = lax.dynamic_slice_in_dim(segment_ids, first_row, TOK_DEV, 0)
        window_keys = lax.dynamic_slice_in_dim(pad_keys, first_row, back_span + TOK_DEV, 0)
        window_values = lax.dynamic_slice_in_dim(pad_values, first_row, back_span + TOK_DEV, 0)
        window_valid = lax.dynamic_slice_in_dim(pad_valid, first_row, back_span + TOK_DEV, 0) > 0
        window_segments = lax.dynamic_slice_in_dim(pad_segments, first_row, back_span + TOK_DEV, 0)
        key_index = first_row - back_span + jnp.arange(back_span + TOK_DEV, dtype=jnp.int32)
        query_index = first_row + jnp.arange(TOK_DEV, dtype=jnp.int32)
        near_mask = window_valid[None, :] & (key_index[None, :] <= query_index[:, None]) & (window_segments[None, :] == query_segments[:, None])
        far_mask = prompt_valid[None, :] & (prompt_segments[None, :] == 0) & (query_segments[:, None] != 0)
        visible = jnp.concatenate([far_mask, near_mask], axis=1)
        context = softmax_context(query_block, jnp.concatenate([prompt_keys, window_keys]), jnp.concatenate([prompt_values, window_values]), visible)
        return jnp.where(query_valid[:, None], context, 0.0)

    devices = jnp.arange(TOKENS // TOK_DEV, dtype=jnp.int32)
    return lax.map(one_stretch, devices).reshape(TOKENS, D)


def reference(hidden_in, query_rows, key_rows, value_rows, stretch_len, segment_ids):
    slot_index = jnp.arange(TOKENS, dtype=jnp.int32)
    slot_valid = ((slot_index % TOK_DEV) < stretch_len[slot_index // TOK_DEV]).astype(jnp.int32)
    first_context = section_layer(query_rows[0], key_rows[0], value_rows[0], slot_valid, segment_ids)
    layer_one = (hidden_in.astype(jnp.float32) + first_context).astype(jnp.bfloat16)
    second_context = section_layer(query_rows[1], key_rows[1], value_rows[1], slot_valid, segment_ids)
    layer_two = (layer_one.astype(jnp.float32) + second_context).astype(jnp.bfloat16)
    return jnp.stack([layer_one, layer_two])
```

```python
import functools
import math

import jax
import jax.numpy as jnp
from jax import lax
from jax.experimental import pallas as pl
from jax.experimental.pallas import tpu as pltpu
from jax.sharding import PartitionSpec as P

D = 8192
QH = 64
KVH = 8
HD = 128
REACH = 6
TOK = 256
PROMPT = 128
GROUP = QH // KVH
PIECES = 2 * KVH
KEYS = PROMPT + (REACH + 1) * TOK
NEG_FILL = -1e30
SCALE = HD ** (-0.5) * math.log2(math.e)
MESH = pl.DeviceIdType.MESH

ROUTES = {
    0: {4: "zy", 3: "xx", 2: "yy", 1: "xy", 6: "zz", 5: "zz"},
    1: {1: "xx", 5: "xx", 4: "zz", 3: "yy", 2: "yy", 6: "zz"},
    2: {2: "yy", 1: "xx", 6: "yz", 5: "zz", 4: "zz", 3: "xx"},
    3: {3: "xx", 2: "yy", 1: "xx", 6: "yy", 5: "zz", 4: "zz"},
}


def upstream(c, way):
    if way == "z":
        return c, 4
    other = c ^ (1 if way == "x" else 2)
    return other, c - other


def stage_of(c, k, kv):
    if k == 0:
        return 0
    other, delta = upstream(c, ROUTES[c][k][kv])
    return stage_of(other, k - delta, kv) + 1


def sends_of(c, kv):
    found = []
    for target in range(4):
        for k, ways in ROUTES[target].items():
            other, delta = upstream(target, ways[kv])
            if other == c:
                found.append((delta, k - delta, k, stage_of(c, k - delta, kv)))
    return found


SENDS = {(c, kv): sends_of(c, kv) for c in range(4) for kv in range(2)}
MAX_SENDS = max(len(v) for v in SENDS.values())
LAST_STAGE = max(stage_of(c, k, kv) for c in range(4) for k in ROUTES[c] for kv in range(2))


def rows_of(k):
    return pl.ds(PROMPT + (REACH - k) * TOK, TOK)


def kernel(n, hidden_ref, q_ref, k_ref, v_ref, len_ref, seg_ref, out_ref,
           buf, qbuf, hbuf, obuf, cbuf, bias, segs,
           load_sem, q_sem, h_sem, o_sem, send_sem, recv_sem, psend_sem, precv_sem,
           seg_send, seg_recv, pass_send):
    me = lax.axis_index("ctx")
    section = lax.axis_index("section")
    c = lax.rem(me, 4)
    z = me // 4
    planes = n // 4
    prompt_lag = planes + 1
    lag = max(LAST_STAGE - 1, prompt_lag)

    def load(i):
        h, kv = i // 2, i % 2
        source = (k_ref, v_ref)[kv]
        return pltpu.make_async_copy(
            source.at[0, :, pl.ds(h * HD, HD)], buf.at[i, rows_of(0)], load_sem.at[i])

    def q_load(h):
        return pltpu.make_async_copy(
            q_ref.at[0, :, pl.ds(pl.multiple_of(h * GROUP * HD, GROUP * HD), GROUP * HD)],
            qbuf.at[h], q_sem.at[h])

    def hidden_load(h):
        return pltpu.make_async_copy(
            hidden_ref.at[:, pl.ds(pl.multiple_of(h * GROUP * HD, GROUP * HD), GROUP * HD)],
            hbuf.at[h], h_sem.at[h])

    def out_store(h):
        return pltpu.make_async_copy(
            obuf.at[h],
            out_ref.at[0, :, pl.ds(pl.multiple_of(h * GROUP * HD, GROUP * HD), GROUP * HD)],
            o_sem.at[h])

    def hand_over(h):
        return pltpu.make_async_remote_copy(
            src_ref=obuf.at[h], dst_ref=hbuf.at[h], send_sem=pass_send.at[h],
            recv_sem=h_sem.at[h], device_id={"section": 1 - section}, device_id_type=MESH)

    def block_copy(i, slot, delta, k_from, k_to):
        return pltpu.make_async_remote_copy(
            src_ref=buf.at[i, rows_of(k_from)], dst_ref=buf.at[i, rows_of(k_to)],
            send_sem=send_sem.at[slot, i], recv_sem=recv_sem.at[k_to - 1, i],
            device_id={"ctx": me + delta}, device_id_type=MESH)

    def prompt_copy(i, slot, delta, source):
        return pltpu.make_async_remote_copy(
            src_ref=buf.at[i, source], dst_ref=buf.at[i, pl.ds(0, PROMPT)],
            send_sem=psend_sem.at[slot, i], recv_sem=precv_sem.at[i],
            device_id={"ctx": me + delta}, device_id_type=MESH)

    def seg_copy(k):
        return pltpu.make_async_remote_copy(
            src_ref=segs.at[0], dst_ref=segs.at[k], send_sem=seg_send.at[k - 1],
            recv_sem=seg_recv.at[k - 1], device_id={"ctx": me + k}, device_id_type=MESH)

    for i in range(PIECES):
        load(i).start()
    segs[0] = seg_ref[...]

    barrier = pltpu.get_barrier_semaphore()
    pl.semaphore_signal(barrier, inc=1, device_id={"section": 1 - section}, device_id_type=MESH)
    for k in range(1, REACH + 1):
        @pl.when(me + k < n)
        def _():
            pl.semaphore_signal(barrier, inc=1, device_id={"ctx": me + k}, device_id_type=MESH)

        @pl.when(me - k >= 0)
        def _():
            pl.semaphore_signal(barrier, inc=1, device_id={"ctx": me - k}, device_id_type=MESH)
    pl.semaphore_wait(barrier, 1 + jnp.minimum(REACH, me) + jnp.minimum(REACH, n - 1 - me))

    for k in range(1, REACH + 1):
        @pl.when(me + k < n)
        def _():
            seg_copy(k).start()

    takes_prompt = (me == 5) | (me >= 7)
    prompt_stage = z + 1 + jnp.where(c == 1, 0, jnp.where(c == 2, 2, 1))
    prompt_sends = {
        1: [(4, lambda: z + 1 < planes), (-1, lambda: z >= 2), (2, lambda: z >= 1)],
        0: [(2, lambda: z >= 2)],
    }

    def each_send(cc, kv, action, stages, i):
        for slot, (delta, k_from, k_to, stage) in enumerate(SENDS[cc, kv]):
            if stage not in stages:
                continue
            good = me >= k_from
            if delta == 4:
                good = good & (z + 1 < planes)

            @pl.when(good)
            def _():
                action(block_copy(i, slot, delta, k_from, k_to))

    def at_corner(cc, body):
        @pl.when(c == cc)
        def _():
            body(cc)

    def own_sends(i):
        kv = i % 2
        load(i).wait()
        for cc in range(4):
            at_corner(cc, lambda cc: each_send(cc, kv, lambda x: x.start(), (0,), i))

    for i in range(PIECES):
        own_sends(i)

    for h in range(KVH):
        q_load(h).start()

    @pl.when(section == 0)
    def _():
        for h in range(KVH):
            hidden_load(h).start()

    for k in range(1, REACH + 1):
        @pl.when(me < k)
        def _():
            @pl.loop(0, PIECES)
            def _(i):
                buf[i, rows_of(k)] = jnp.zeros((TOK, HD), jnp.bfloat16)
            segs[k] = jnp.zeros((1, TOK), jnp.int32)

    for k in range(1, REACH + 1):
        @pl.when(me >= k)
        def _():
            seg_copy(k).wait_recv()

    own_row = segs[0]
    row = lax.broadcasted_iota(jnp.int32, (TOK, TOK), 0)
    col = lax.broadcasted_iota(jnp.int32, (TOK, TOK), 1)
    own_col = jnp.sum(
        jnp.where(row == col, jnp.broadcast_to(own_row, (TOK, TOK)), 0).astype(jnp.float32),
        axis=1, keepdims=True).astype(jnp.int32)
    bias[:, :PROMPT] = jnp.broadcast_to(
        jnp.where(own_col != 0, 0.0, NEG_FILL), (TOK, PROMPT)).astype(jnp.float32)
    for k in range(REACH + 1):
        filled = jnp.where(me >= k, len_ref[jnp.maximum(me - k, 0)], 0)
        seen = (col < filled) & (segs[k] == own_col)
        if k == 0:
            seen = seen & (col <= row)
        bias[:, PROMPT + (REACH - k) * TOK:PROMPT + (REACH - k + 1) * TOK] = jnp.where(
            seen, 0.0, NEG_FILL)
    query_len = len_ref[me]

    def communicate(p, parity):
        for stage in range(1, LAST_STAGE + 1):
            i = p - (stage - 1)
            kv = (parity - (stage - 1)) % 2

            @pl.when((i >= 0) & (i < PIECES))
            def _():
                def relay(cc):
                    for k in ROUTES[cc]:
                        if stage_of(cc, k, kv) != stage:
                            continue

                        @pl.when(me >= k)
                        def _():
                            block_copy(i, 0, 0, 0, k).wait_recv()
                    each_send(cc, kv, lambda x: x.start(), (stage,), i)
                for cc in range(4):
                    at_corner(cc, relay)

        j = p - (prompt_stage - 1)
        good = (j >= 0) & (j < PIECES)

        @pl.when(good & takes_prompt)
        def _():
            prompt_copy(j, 0, 0, pl.ds(0, PROMPT)).wait_recv()

        for cc, targets in prompt_sends.items():
            for slot, (delta, rule) in enumerate(targets):
                @pl.when(good & (c == cc) & (z >= 1) & rule())
                def _():
                    prompt_copy(j, slot, delta, pl.ds(0, PROMPT)).start()

        @pl.when(good & (me == 1))
        def _():
            prompt_copy(j, 0, 4, pl.ds(PROMPT + (REACH - 1) * TOK, PROMPT)).start()

    valid = lax.broadcasted_iota(jnp.int32, (TOK, HD), 0) < query_len

    def heads(h, first, count):
        @pl.loop(first, first + count)
        def _(g):
            lanes = pl.ds(pl.multiple_of(g * HD, HD), HD)
            scores = lax.dot_general(
                qbuf[h, :, lanes], buf[2 * h], (((1,), (1,)), ((), ())),
                preferred_element_type=jnp.float32)
            scores = scores * SCALE + bias[...]
            top = jnp.max(scores, axis=1, keepdims=True)
            weights = jnp.exp2(scores - top).astype(jnp.bfloat16)
            values = jnp.concatenate(
                [buf[2 * h + 1], jnp.ones((KEYS, HD), jnp.bfloat16)], axis=1)
            mixed = jnp.dot(weights, values, preferred_element_type=jnp.float32)
            cbuf[h, :, lanes] = jnp.where(valid, mixed[:, :HD] / mixed[:, HD:], 0.0)

    def finish(h):
        @pl.loop(0, GROUP)
        def _(g):
            lanes = pl.ds(pl.multiple_of(g * HD, HD), HD)
            obuf[h, :, lanes] = (
                hbuf[h, :, lanes].astype(jnp.float32) + cbuf[h, :, lanes]).astype(jnp.bfloat16)
        out_store(h).start()

    def finish_first(h):
        hidden_load(h).wait()
        finish(h)
        hand_over(h).start()

    def finish_second(h):
        hand_over(h).wait_recv()
        finish(h)

    @pl.loop(0, (lag + 1) // 2 + KVH + 1)
    def _(t):
        start_phase = (lag + 1) // 2
        for parity in range(2):
            communicate(2 * t + parity, parity)
            half = (parity + lag + 1) % 2
            h = t - start_phase - (1 if lag % 2 == 0 and half == 1 else 0)

            @pl.when((h >= 0) & (h < KVH))
            def _():
                if half == 0:
                    q_load(h).wait()

                    @pl.when((me < 5) | (me == 6))
                    def _():
                        block0 = pl.ds(
                            pl.multiple_of(PROMPT + (REACH - me) * TOK, PROMPT), PROMPT)
                        buf[2 * h, :PROMPT] = buf[2 * h, block0]
                        buf[2 * h + 1, :PROMPT] = buf[2 * h + 1, block0]
                heads(h, half * (GROUP // 2), GROUP // 2)
                if half == 1:
                    @pl.when(section == 0)
                    def _():
                        finish_first(h)

                    @pl.when((section == 1) & (h >= 1))
                    def _():
                        finish_second(h - 1)

    @pl.when(section == 1)
    def _():
        finish_second(KVH - 1)

    for k in range(1, REACH + 1):
        @pl.when(me + k < n)
        def _():
            seg_copy(k).wait_send()

    @pl.loop(0, KVH)
    def _(h):
        out_store(h).wait()

        @pl.when(section == 0)
        def _():
            hand_over(h).wait_send()
        for kv in range(2):
            i = 2 * h + kv
            for cc in range(4):
                at_corner(cc, lambda cc: each_send(
                    cc, kv, lambda x: x.wait_send(), range(LAST_STAGE + 1), i))
            for cc, targets in prompt_sends.items():
                for slot, (delta, rule) in enumerate(targets):
                    @pl.when((c == cc) & (z >= 1) & rule())
                    def _():
                        prompt_copy(i, slot, delta, pl.ds(0, PROMPT)).wait_send()

            @pl.when(me == 1)
            def _():
                prompt_copy(i, 0, 4, pl.ds(0, PROMPT)).wait_send()


def local(n, hidden_in, query_rows, key_rows, value_rows, stretch_len, segment_ids):
    anywhere = pl.BlockSpec(memory_space=pl.ANY)
    wide = GROUP * HD
    dma = pltpu.SemaphoreType.DMA
    return pl.pallas_call(
        functools.partial(kernel, n),
        out_shape=jax.ShapeDtypeStruct((1, TOK, D), jnp.bfloat16),
        in_specs=[anywhere] * 4 + [
            pl.BlockSpec(memory_space=pltpu.SMEM), pl.BlockSpec(memory_space=pltpu.VMEM)],
        out_specs=anywhere,
        scratch_shapes=[
            pltpu.VMEM((PIECES, KEYS, HD), jnp.bfloat16),
            pltpu.VMEM((KVH, TOK, wide), jnp.bfloat16),
            pltpu.VMEM((KVH, TOK, wide), jnp.bfloat16),
            pltpu.VMEM((KVH, TOK, wide), jnp.bfloat16),
            pltpu.VMEM((KVH, TOK, wide), jnp.float32),
            pltpu.VMEM((TOK, KEYS), jnp.float32),
            pltpu.VMEM((REACH + 1, 1, TOK), jnp.int32),
            dma((PIECES,)),
            dma((KVH,)),
            dma((KVH,)),
            dma((KVH,)),
            dma((MAX_SENDS, PIECES)),
            dma((REACH, PIECES)),
            dma((3, PIECES)),
            dma((PIECES,)),
            dma((REACH,)),
            dma((REACH,)),
            dma((KVH,)),
        ],
        compiler_params=pltpu.CompilerParams(
            collective_id=0, has_side_effects=True, vmem_limit_bytes=56 * 1024 * 1024),
    )(hidden_in, query_rows, key_rows, value_rows, stretch_len, segment_ids.reshape(1, TOK))


def solution(mesh):
    return jax.shard_map(
        functools.partial(local, mesh.shape["ctx"]),
        mesh=mesh,
        in_specs=(
            P("ctx", None),
            P("section", "ctx", None),
            P("section", "ctx", None),
            P("section", "ctx", None),
            P(),
            P("ctx"),
        ),
        out_specs=P("section", "ctx", None),
        check_vma=False,
    )
```

```python
import functools
import math

import jax
import jax.numpy as jnp
from jax import lax
from jax.experimental import pallas as pl
from jax.experimental.pallas import tpu as pltpu
from jax.sharding import PartitionSpec as P

D = 8192
QH = 64
KVH = 8
HD = 128
REACH = 6
TOK = 256
PROMPT = 128
GROUP = QH // KVH
PIECES = 2 * KVH
KEYS = PROMPT + (REACH + 1) * TOK
NEG_FILL = -1e30
LEAD = 2
SCALE = HD ** (-0.5) * math.log2(math.e)
MESH = pl.DeviceIdType.MESH

ROUTES = {
    0: {4: "zy", 3: "xx", 2: "yy", 1: "xy", 6: "zz", 5: "zz"},
    1: {1: "xx", 5: "xx", 4: "zz", 3: "yy", 2: "yy", 6: "zz"},
    2: {2: "yy", 1: "xx", 6: "yz", 5: "zz", 4: "zz", 3: "xx"},
    3: {3: "xx", 2: "yy", 1: "xx", 6: "yy", 5: "zz", 4: "zz"},
}


def upstream(c, way):
    if way == "z":
        return c, 4
    other = c ^ (1 if way == "x" else 2)
    return other, c - other


def stage_of(c, k, kv):
    if k == 0:
        return 0
    other, delta = upstream(c, ROUTES[c][k][kv])
    return stage_of(other, k - delta, kv) + 1


def sends_of(c, kv):
    found = []
    for target in range(4):
        for k, ways in ROUTES[target].items():
            other, delta = upstream(target, ways[kv])
            if other == c:
                found.append((delta, k - delta, k, stage_of(c, k - delta, kv)))
    return found


SENDS = {(c, kv): sends_of(c, kv) for c in range(4) for kv in range(2)}
MAX_SENDS = max(len(v) for v in SENDS.values())
LAST_STAGE = max(stage_of(c, k, kv) for c in range(4) for k in ROUTES[c] for kv in range(2))


def rows_of(k):
    return pl.ds(PROMPT + (REACH - k) * TOK, TOK)


def kernel(n, hidden_ref, q_ref, k_ref, v_ref, len_ref, seg_ref, out_ref,
           buf, qbuf, hbuf, obuf, cbuf, bias, segs,
           load_sem, q_sem, h_sem, o_sem, send_sem, recv_sem, psend_sem, precv_sem,
           seg_send, seg_recv, pass_send):
    me = lax.axis_index("ctx")
    section = lax.axis_index("section")
    c = lax.rem(me, 4)
    z = me // 4
    planes = n // 4
    prompt_lag = planes + 1
    lag = max(LAST_STAGE - 1, prompt_lag)

    def load(i, kv):
        source = (k_ref, v_ref)[kv]
        return pltpu.make_async_copy(
            source.at[0, :, pl.ds(pl.multiple_of((i // 2) * HD, HD), HD)], buf.at[i, rows_of(0)], load_sem.at[i])

    def q_load(h):
        return pltpu.make_async_copy(
            q_ref.at[0, :, pl.ds(pl.multiple_of(h * GROUP * HD, GROUP * HD), GROUP * HD)],
            qbuf.at[h], q_sem.at[h])

    def hidden_load(h):
        return pltpu.make_async_copy(
            hidden_ref.at[:, pl.ds(pl.multiple_of(h * GROUP * HD, GROUP * HD), GROUP * HD)],
            hbuf.at[h], h_sem.at[h])

    def out_store(h):
        return pltpu.make_async_copy(
            obuf.at[h],
            out_ref.at[0, :, pl.ds(pl.multiple_of(h * GROUP * HD, GROUP * HD), GROUP * HD)],
            o_sem.at[h])

    def hand_over(h):
        return pltpu.make_async_remote_copy(
            src_ref=obuf.at[h], dst_ref=hbuf.at[h], send_sem=pass_send.at[h],
            recv_sem=h_sem.at[h], device_id={"section": 1 - section}, device_id_type=MESH)

    def block_copy(i, slot, delta, k_from, k_to):
        return pltpu.make_async_remote_copy(
            src_ref=buf.at[i, rows_of(k_from)], dst_ref=buf.at[i, rows_of(k_to)],
            send_sem=send_sem.at[slot, i], recv_sem=recv_sem.at[k_to - 1, i],
            device_id={"ctx": me + delta}, device_id_type=MESH)

    def prompt_copy(i, slot, delta, source):
        return pltpu.make_async_remote_copy(
            src_ref=buf.at[i, source], dst_ref=buf.at[i, pl.ds(0, PROMPT)],
            send_sem=psend_sem.at[slot, i], recv_sem=precv_sem.at[i],
            device_id={"ctx": me + delta}, device_id_type=MESH)

    def seg_copy(k):
        return pltpu.make_async_remote_copy(
            src_ref=segs.at[0], dst_ref=segs.at[k], send_sem=seg_send.at[k - 1],
            recv_sem=seg_recv.at[k - 1], device_id={"ctx": me + k}, device_id_type=MESH)

    for i in range(PIECES):
        load(i, i % 2).start()
    segs[0] = seg_ref[...]

    barrier = pltpu.get_barrier_semaphore()
    pl.semaphore_signal(barrier, inc=1, device_id={"section": 1 - section}, device_id_type=MESH)
    for k in range(1, REACH + 1):
        @pl.when(me + k < n)
        def _():
            pl.semaphore_signal(barrier, inc=1, device_id={"ctx": me + k}, device_id_type=MESH)

        @pl.when(me - k >= 0)
        def _():
            pl.semaphore_signal(barrier, inc=1, device_id={"ctx": me - k}, device_id_type=MESH)
    pl.semaphore_wait(barrier, 1 + jnp.minimum(REACH, me) + jnp.minimum(REACH, n - 1 - me))

    for k in range(1, REACH + 1):
        @pl.when(me + k < n)
        def _():
            seg_copy(k).start()

    takes_prompt = (me == 5) | (me >= 7)
    prompt_stage = z + 1 + jnp.where(c == 1, 0, jnp.where(c == 2, 2, 1))
    prompt_sends = {
        1: [(4, lambda: z + 1 < planes), (-1, lambda: z >= 2), (2, lambda: z >= 1)],
        0: [(2, lambda: z >= 2)],
    }

    def each_send(cc, kv, action, stages, i):
        for slot, (delta, k_from, k_to, stage) in enumerate(SENDS[cc, kv]):
            if stage not in stages:
                continue
            good = me >= k_from
            if delta == 4:
                good = good & (z + 1 < planes)

            @pl.when(good)
            def _():
                action(block_copy(i, slot, delta, k_from, k_to))

    def at_corner(cc, body):
        @pl.when(c == cc)
        def _():
            body(cc)

    def own_sends(i, kv):
        load(i, kv).wait()
        for cc in range(4):
            at_corner(cc, lambda cc: each_send(cc, kv, lambda x: x.start(), (0,), i))

    for i in range(LEAD):
        own_sends(i, i % 2)

    for h in range(KVH):
        q_load(h).start()

    @pl.when(section == 0)
    def _():
        for h in range(KVH):
            hidden_load(h).start()

    for k in range(1, REACH + 1):
        @pl.when(me < k)
        def _():
            @pl.loop(0, PIECES)
            def _(i):
                buf[i, rows_of(k)] = jnp.zeros((TOK, HD), jnp.bfloat16)
            segs[k] = jnp.zeros((1, TOK), jnp.int32)

    for k in range(1, REACH + 1):
        @pl.when(me >= k)
        def _():
            seg_copy(k).wait_recv()

    own_row = segs[0]
    row = lax.broadcasted_iota(jnp.int32, (TOK, TOK), 0)
    col = lax.broadcasted_iota(jnp.int32, (TOK, TOK), 1)
    own_col = jnp.sum(
        jnp.where(row == col, jnp.broadcast_to(own_row, (TOK, TOK)), 0).astype(jnp.float32),
        axis=1, keepdims=True).astype(jnp.int32)
    bias[:, :PROMPT] = jnp.broadcast_to(
        jnp.where(own_col != 0, 0.0, NEG_FILL), (TOK, PROMPT)).astype(jnp.float32)
    for k in range(REACH + 1):
        filled = jnp.where(me >= k, len_ref[jnp.maximum(me - k, 0)], 0)
        seen = (col < filled) & (segs[k] == own_col)
        if k == 0:
            seen = seen & (col <= row)
        bias[:, PROMPT + (REACH - k) * TOK:PROMPT + (REACH - k + 1) * TOK] = jnp.where(
            seen, 0.0, NEG_FILL)
    query_len = len_ref[me]

    def communicate(p, parity):
        @pl.when(p + LEAD < PIECES)
        def _():
            own_sends(p + LEAD, (parity + LEAD) % 2)

        for stage in range(1, LAST_STAGE + 1):
            i = p - (stage - 1)
            kv = (parity - (stage - 1)) % 2

            @pl.when((i >= 0) & (i < PIECES))
            def _():
                def relay(cc):
                    for k in ROUTES[cc]:
                        if stage_of(cc, k, kv) != stage:
                            continue

                        @pl.when(me >= k)
                        def _():
                            block_copy(i, 0, 0, 0, k).wait_recv()
                    each_send(cc, kv, lambda x: x.start(), (stage,), i)
                for cc in range(4):
                    at_corner(cc, relay)

        j = p - (prompt_stage - 1)
        good = (j >= 0) & (j < PIECES)

        @pl.when(good & takes_prompt)
        def _():
            prompt_copy(j, 0, 0, pl.ds(0, PROMPT)).wait_recv()

        for cc, targets in prompt_sends.items():
            for slot, (delta, rule) in enumerate(targets):
                @pl.when(good & (c == cc) & (z >= 1) & rule())
                def _():
                    prompt_copy(j, slot, delta, pl.ds(0, PROMPT)).start()

        @pl.when(good & (me == 1))
        def _():
            prompt_copy(j, 0, 4, pl.ds(PROMPT + (REACH - 1) * TOK, PROMPT)).start()

    valid = lax.broadcasted_iota(jnp.int32, (TOK, HD), 0) < query_len

    def heads(h, first, count):
        def scores_of(g):
            scores = lax.dot_general(
                qbuf[h, :, g * HD:(g + 1) * HD], buf[2 * h], (((1,), (1,)), ((), ())),
                preferred_element_type=jnp.float32)
            return scores * SCALE + bias[...]

        all_scores = [scores_of(g) for g in range(first, first + count)]
        for g, scores in zip(range(first, first + count), all_scores):
            top = jnp.max(scores, axis=1, keepdims=True)
            weights = jnp.exp2(scores - top).astype(jnp.bfloat16)
            values = jnp.concatenate(
                [buf[2 * h + 1], jnp.ones((KEYS, HD), jnp.bfloat16)], axis=1)
            mixed = jnp.dot(weights, values, preferred_element_type=jnp.float32)
            cbuf[h, :, g * HD:(g + 1) * HD] = jnp.where(valid, mixed[:, :HD] / mixed[:, HD:], 0.0)

    def finish(h):
        @pl.loop(0, GROUP)
        def _(g):
            lanes = pl.ds(pl.multiple_of(g * HD, HD), HD)
            obuf[h, :, lanes] = (
                hbuf[h, :, lanes].astype(jnp.float32) + cbuf[h, :, lanes]).astype(jnp.bfloat16)
        out_store(h).start()

    def finish_first(h):
        hidden_load(h).wait()
        finish(h)
        hand_over(h).start()

    def finish_second(h):
        hand_over(h).wait_recv()
        finish(h)

    @pl.loop(0, (lag + 1) // 2 + KVH + 1)
    def _(t):
        start_phase = (lag + 1) // 2
        for parity in range(2):
            communicate(2 * t + parity, parity)
            half = (parity + lag + 1) % 2
            h = t - start_phase - (1 if lag % 2 == 0 and half == 1 else 0)

            @pl.when((h >= 0) & (h < KVH))
            def _():
                if half == 0:
                    q_load(h).wait()

                    @pl.when((me < 5) | (me == 6))
                    def _():
                        block0 = pl.ds(
                            pl.multiple_of(PROMPT + (REACH - me) * TOK, PROMPT), PROMPT)
                        buf[2 * h, :PROMPT] = buf[2 * h, block0]
                        buf[2 * h + 1, :PROMPT] = buf[2 * h + 1, block0]
                heads(h, half * (GROUP // 2), GROUP // 2)
                if half == 1:
                    @pl.when(section == 0)
                    def _():
                        finish_first(h)

                    @pl.when((section == 1) & (h >= 1))
                    def _():
                        finish_second(h - 1)

    @pl.when(section == 1)
    def _():
        finish_second(KVH - 1)

    for k in range(1, REACH + 1):
        @pl.when(me + k < n)
        def _():
            seg_copy(k).wait_send()

    @pl.loop(0, KVH)
    def _(h):
        out_store(h).wait()

        @pl.when(section == 0)
        def _():
            hand_over(h).wait_send()
        for kv in range(2):
            i = 2 * h + kv
            for cc in range(4):
                at_corner(cc, lambda cc: each_send(
                    cc, kv, lambda x: x.wait_send(), range(LAST_STAGE + 1), i))
            for cc, targets in prompt_sends.items():
                for slot, (delta, rule) in enumerate(targets):
                    @pl.when((c == cc) & (z >= 1) & rule())
                    def _():
                        prompt_copy(i, slot, delta, pl.ds(0, PROMPT)).wait_send()

            @pl.when(me == 1)
            def _():
                prompt_copy(i, 0, 4, pl.ds(0, PROMPT)).wait_send()


def local(n, hidden_in, query_rows, key_rows, value_rows, stretch_len, segment_ids):
    anywhere = pl.BlockSpec(memory_space=pl.ANY)
    wide = GROUP * HD
    dma = pltpu.SemaphoreType.DMA
    return pl.pallas_call(
        functools.partial(kernel, n),
        out_shape=jax.ShapeDtypeStruct((1, TOK, D), jnp.bfloat16),
        in_specs=[anywhere] * 4 + [
            pl.BlockSpec(memory_space=pltpu.SMEM), pl.BlockSpec(memory_space=pltpu.VMEM)],
        out_specs=anywhere,
        scratch_shapes=[
            pltpu.VMEM((PIECES, KEYS, HD), jnp.bfloat16),
            pltpu.VMEM((KVH, TOK, wide), jnp.bfloat16),
            pltpu.VMEM((KVH, TOK, wide), jnp.bfloat16),
            pltpu.VMEM((KVH, TOK, wide), jnp.bfloat16),
            pltpu.VMEM((KVH, TOK, wide), jnp.float32),
            pltpu.VMEM((TOK, KEYS), jnp.float32),
            pltpu.VMEM((REACH + 1, 1, TOK), jnp.int32),
            dma((PIECES,)),
            dma((KVH,)),
            dma((KVH,)),
            dma((KVH,)),
            dma((MAX_SENDS, PIECES)),
            dma((REACH, PIECES)),
            dma((3, PIECES)),
            dma((PIECES,)),
            dma((REACH,)),
            dma((REACH,)),
            dma((KVH,)),
        ],
        compiler_params=pltpu.CompilerParams(
            collective_id=0, has_side_effects=True, vmem_limit_bytes=56 * 1024 * 1024),
    )(hidden_in, query_rows, key_rows, value_rows, stretch_len, segment_ids.reshape(1, TOK))


def solution(mesh):
    return jax.shard_map(
        functools.partial(local, mesh.shape["ctx"]),
        mesh=mesh,
        in_specs=(
            P("ctx", None),
            P("section", "ctx", None),
            P("section", "ctx", None),
            P("section", "ctx", None),
            P(),
            P("ctx"),
        ),
        out_specs=P("section", "ctx", None),
        check_vma=False,
    )
```
